128 devices in a mesh: row: 4 (over x), col: 32 (over y, z, core).
Axes of the slice: x: 4, y: 4, z: 4, core: 2. Of those that a mesh axis runs over, the one named last changes fastest.
Arguments:
- trailing: float32 [15360, 15360], P('row', 'col'), as said below
- first_panel: float32 [15360, 512], P(('row', 'col')), may hold values from -0.046875 to 0.046875
- first_gram: float32 [512, 512], replicated, as said below
- second_panel: float32 [15360, 512], P(('row', 'col')), may hold values from -0.046875 to 0.046875
- second_lead: float32 [512, 512], replicated, may hold values from -0.046875 to 0.046875
- second_gram: float32 [512, 512], replicated, as said below
- tile_owner: int32 [24576, 1], P(('row', 'col')), may hold values from 0 to 127; in each aligned block of 192 rows (0 to 191, 192 to 383, ...) at most 2 rows name the same one
- tile_rows: int32 [24576, 128], P(('row', 'col')), may hold values from -1 to 479, as said below
- tile_block: int32 [24576], P(('row', 'col')), may hold values from 0 to 3
- tile_count: int32 [128], P(('row', 'col')), may hold values from 144 to 192
Outputs:
- first_column: float32 [15360, 512], P('col')
- first_corner: float32 [512, 512], P('col')
- second_upper: float32 [512, 512], P('col')
- second_column: float32 [15360, 512], P('col')
- second_corner: float32 [512, 512], P('col')
- child_tiles: bfloat16 [32768, 128, 128], P(('row', 'col'))
The draws below stay inside these ranges and needn't reach their ends.
Inputs may be any that keep to these rules, and one draw needn't show every extreme that they name: trailing is exactly symmetric. first_gram is exactly symmetric. second_gram is exactly symmetric. `tile_owner`: among the tiles of one device no owner is named more than 2 times. `tile_rows`: in each tile the live indices come first and the rest are -1; a live index points into the sender's own block of 15360 / (devices along col) rows.
All inputs are finite; a program needn't handle non-finite values.
Results may differ from the reference program's by a relative error of at most 0.012.
Values may be sent and summed in bfloat16 or wider, within the bound.
No kernel may reach another device: no remote copies, remote signals or barrier semaphores. Data moves between devices by JAX's collectives and lax.ppermute only.
A program may use at most 192 MiB of HBM per device.

```python
import math
import jax
import jax.numpy as jnp
import numpy as np
from jax import lax

P_SIZE = 512
TILE = 128
TILE_CAP = 2
M = 15360
TILES_DEV = 192
N_COL = 32
DEVICES = 128


def symmetric_dominant(key, order):
    first_key, second_key = jax.random.split(key)
    raw = jax.random.normal(first_key, (order, order), jnp.float32)
    symmetric = (raw + raw.T) * 0.70710678
    diagonal = M ** 0.5 * jax.random.uniform(second_key, (order,), jnp.float32, 1.0, 2.0)
    positions = jnp.arange(order)
    return symmetric.at[positions, positions].add(diagonal)


def draw_trailing(key, part):
    key = jax.random.fold_in(key, 1)
    return symmetric_dominant(key, M)


def draw_first_gram(key, part):
    key = jax.random.fold_in(key, 2)
    return symmetric_dominant(key, P_SIZE)


def draw_second_gram(key, part):
    key = jax.random.fold_in(key, 3)
    return symmetric_dominant(key, P_SIZE)


def draw_tile_rows(key, part):
    key = jax.random.fold_in(key, 11)
    first_key, second_key = jax.random.split(key)
    total = DEVICES * TILES_DEV
    picks = jax.random.randint(first_key, (total, TILE), 0, M // N_COL)
    within = jnp.arange(total) % TILES_DEV
    picks = jnp.where((within[:, None] == 0) & (jnp.arange(TILE)[None, :] == 0), M // N_COL - 1, picks)
    lengths = jax.random.randint(second_key, (total,), TILE // 2, TILE + 1)
    lengths = jnp.where(within == 0, TILE, jnp.where(within == 1, TILE // 2, lengths))
    return jnp.where(jnp.arange(TILE)[None, :] < lengths[:, None], picks, -1).astype(jnp.int32)


def draw_tile_count(key, part):
    key = jax.random.fold_in(key, 12)
    first_key, second_key = jax.random.split(key)
    counts = jax.random.randint(first_key, (DEVICES,), 3 * TILES_DEV // 4, TILES_DEV + 1)
    spot = jax.random.randint(second_key, (), 0, DEVICES)
    other = (spot + 1) % DEVICES
    positions = jnp.arange(DEVICES)
    counts = jnp.where(positions == spot, TILES_DEV, counts)
    counts = jnp.where(positions == other, 3 * TILES_DEV // 4, counts)
    return counts.astype(jnp.int32)


def place_ends(entries, key, least, high):
    longest = entries.shape.index(max(entries.shape))
    spots = []
    for shift in (0, 1):
        where = [jax.random.randint(jax.random.fold_in(key, axis), (), 0, length) for axis, length in enumerate(entries.shape)]
        where[longest] = (where[longest] + shift) % entries.shape[longest]
        spots.append(tuple(where))
    return entries.at[spots[0]].set(least).at[spots[1]].set(high)


def level_of(key, dims, shards, smallest, high):
    def one(position, parts):
        draws = jax.random.uniform(jax.random.fold_in(jax.random.fold_in(key, 6), position), (parts,), jnp.float32, smallest / len(shards), high / len(shards))
        return jnp.repeat(jnp.exp(draws), dims[position] // parts).reshape((-1,) + (1,) * (len(dims) - position - 1))

    factor_of = one(*shards[0])
    for cut in shards[1:]:
        factor_of = factor_of * one(*cut)
    return factor_of


def shared_out(own_key, own, number, rows, number_of, top, limit, skew):
    order = jax.random.permutation(own_key, number_of)
    crowded, usual = portions_of(number_of, rows * top, limit, skew, True), portions_of(number_of, rows * top, limit, skew, False)
    places = jnp.arange(number_of)

    def named(tallies, offset_by):
        used = int((tallies > 0).sum())
        fixed = max(1, used // 4)
        passed = fixed + (places - fixed + offset_by * (used - fixed)) % max(1, number_of - fixed)
        return jnp.zeros((number_of,), jnp.int32).at[order[jnp.where(places < fixed, places, passed)]].set(jnp.asarray(tallies, jnp.int32))

    tallies = jnp.where(number % 4 == 0, named(crowded, number // 4), named(usual, number - number // 4 - 1))
    mixed = jax.random.permutation(jax.random.fold_in(own, 3), number_of)
    giver, sink = mixed[0:number_of // 2 * 2:2], mixed[1:number_of // 2 * 2:2]
    margin = jnp.minimum(tallies[giver] - 1, limit - tallies[sink]) // 2
    margin = jnp.where((giver == order[0]) | (sink == order[0]) | (tallies[sink] == 0), 0, jnp.maximum(margin, 0))
    passed = jax.random.randint(jax.random.fold_in(own, 4), (number_of // 2,), 0, 1 << 20) % (margin + 1)
    tallies = tallies.at[giver].add(-passed).at[sink].add(passed)
    labels = jnp.searchsorted(jnp.cumsum(tallies), jnp.arange(rows * top), side="right").astype(jnp.int32)
    grid = labels.reshape(top, rows).T
    grid = grid[jax.random.permutation(jax.random.fold_in(own, 1), rows)]
    offset_by = jax.random.randint(jax.random.fold_in(own, 2), (rows, 1), 0, top)
    return jnp.take_along_axis(grid, (jnp.arange(top)[None, :] + offset_by) % top, axis=1)


def portions_of(amount, total, most, lean, full):
    weights = [(1 << 20) // math.isqrt(rank ** lean) + 1 for rank in range(1, amount + 1)]
    largest = most if full else min(most, max(-(-total // amount), total * weights[0] // sum(weights)))
    least = 1 if total - largest >= amount - 1 else 0
    given, spare = [largest] + [least] * (amount - 1), total - largest - least * (amount - 1)
    while spare > 0:
        free = [i for i in range(1, amount) if given[i] < largest] or [i for i in range(1, amount) if given[i] < most]
        whole, left = sum([weights[i] for i in free]), spare
        for i in free:
            extra = min(most - given[i], max(1, left * weights[i] // whole), spare)
            given[i] = given[i] + extra
            spare = spare - extra
    return np.array(given)


def gaussian(rng, extent, spread, bound, pieces=(), held_as=jnp.bfloat16):
    values = jax.random.normal(rng, extent, jnp.float32) * spread
    if len(pieces) > 0:
        values = level_of(rng, extent, pieces, -0.22, 0.18) * values
    return jnp.clip(values, min=-bound, max=bound).astype(held_as)


def setup_inputs(seed: int = 0) -> dict:
    keys = jax.random.split(jax.random.key(seed), 11)
    trailing = draw_trailing(jax.random.fold_in(keys[10], 71), 0)
    first_panel = gaussian(keys[1], (M, P_SIZE), M ** -0.5, 0.046875, ((0, 128),), jnp.float32)
    first_gram = draw_first_gram(jax.random.fold_in(keys[10], 71), 0)
    second_panel = gaussian(keys[3], (M, P_SIZE), M ** -0.5, 0.046875, ((0, 128),), jnp.float32)
    second_lead = gaussian(keys[4], (P_SIZE, P_SIZE), M ** -0.5, 0.046875, (), jnp.float32)
    second_gram = draw_second_gram(jax.random.fold_in(keys[10], 71), 0)
    tile_owner_keys = jax.random.split(jax.random.fold_in(keys[6], 1), (DEVICES * TILES_DEV) // TILES_DEV)
    tile_owner_turns = jax.random.permutation(jax.random.fold_in(keys[6], 3), (DEVICES * TILES_DEV) // TILES_DEV)
    tile_owner = jax.vmap(lambda own, number: shared_out(jax.random.fold_in(keys[6], 2), own, number, TILES_DEV, DEVICES, 1, TILE_CAP, 2))(tile_owner_keys, tile_owner_turns).reshape((DEVICES * TILES_DEV, 1))
    tile_rows = draw_tile_rows(jax.random.fold_in(keys[10], 71), 0)
    tile_block = place_ends(jax.random.randint(keys[8], (DEVICES * TILES_DEV,), 0, P_SIZE // TILE), jax.random.fold_in(keys[8], 1), 0, (P_SIZE // TILE) - 1).astype(jnp.int32)
    tile_count = draw_tile_count(jax.random.fold_in(keys[10], 71), 0)
    return {"trailing": trailing, "first_panel": first_panel, "first_gram": first_gram, "second_panel": second_panel, "second_lead": second_lead, "second_gram": second_gram, "tile_owner": tile_owner, "tile_rows": tile_rows, "tile_block": tile_block, "tile_count": tile_count}


def multiply(left, right):
    return jnp.dot(left, right, precision=lax.Precision.HIGHEST, preferred_element_type=jnp.float32)


def reference(trailing, first_panel, first_gram, second_panel, second_lead, second_gram, tile_owner, tile_rows, tile_block, tile_count):
    first_column = -multiply(trailing, first_panel)
    first_corner = first_gram - multiply(first_panel.T, first_column)
    second_column = -(multiply(first_column, second_lead) + multiply(trailing, second_panel))
    second_upper = -(multiply(first_corner, second_lead) + multiply(first_column.T, second_panel))
    second_corner = second_gram - (multiply(second_lead.T, second_upper) + multiply(second_panel.T, second_column))

    band_rows = M // N_COL
    blocks_view = second_column.reshape(N_COL, band_rows, P_SIZE // TILE, TILE)

    def make_tiles(sender):
        column = (sender % N_COL).astype(jnp.int32)
        local_view = lax.dynamic_index_in_dim(blocks_view, column, 0, keepdims=False)
        rows_here = lax.dynamic_slice_in_dim(tile_rows, (sender * TILES_DEV).astype(jnp.int32), TILES_DEV, 0)
        blocks_here = lax.dynamic_slice_in_dim(tile_block, (sender * TILES_DEV).astype(jnp.int32), TILES_DEV, 0)
        picked = local_view[jnp.clip(rows_here, 0, band_rows - 1), blocks_here[:, None]]
        return jnp.where(rows_here[:, :, None] >= 0, picked, jnp.float32(0.0)).astype(jnp.bfloat16)

    senders = jnp.arange(DEVICES, dtype=jnp.int32)
    tiles = lax.map(make_tiles, senders)
    owners = tile_owner[:, 0].reshape(DEVICES, TILES_DEV)
    order_ids = jnp.arange(TILES_DEV, dtype=jnp.int32)
    live = order_ids[None, :] < tile_count[:, None]
    earlier = (owners[:, :, None] == owners[:, None, :]) & live[:, None, :] & (order_ids[None, None, :] < order_ids[None, :, None])
    slots = jnp.sum(earlier.astype(jnp.int32), axis=2)
    dump = DEVICES * DEVICES * TILE_CAP
    target = jnp.where(live, (owners * DEVICES + senders[:, None]) * TILE_CAP + slots, dump)
    child_tiles = jnp.zeros((dump + 1, TILE, TILE), jnp.bfloat16).at[target.reshape(-1)].set(tiles.reshape(-1, TILE, TILE))[:dump]
    return first_column, first_corner, second_upper, second_column, second_corner, child_tiles
```

```python
import functools

import jax
import jax.numpy as jnp
from jax import lax
from jax.experimental import pallas as pl
from jax.experimental.pallas import tpu as pltpu
from jax.sharding import PartitionSpec as P

P_SIZE = 512
TILE = 128
TILE_CAP = 2
CODE = 512


def precise(left, right):
    return jnp.dot(left, right, precision=lax.Precision.HIGHEST, preferred_element_type=jnp.float32)


def contract_rows(left, right):
    return lax.dot_general(
        left, right, (((0,), (0,)), ((), ())), preferred_element_type=jnp.float32
    )


def shift_rows(value, step):
    size = lax.axis_size("row")
    return lax.ppermute(value, "row", [(i, (i + step) % size) for i in range(size)])


def spread_rows(block):
    size = lax.axis_size("row")
    row = lax.axis_index("row")
    out = jnp.zeros((size,) + block.shape, block.dtype)
    out = lax.dynamic_update_index_in_dim(out, block, row, 0)
    for step in range(1, size):
        out = lax.dynamic_update_index_in_dim(out, shift_rows(block, step), (row - step) % size, 0)
    return out


def sum_rows(parts):
    size = lax.axis_size("row")
    row = lax.axis_index("row")
    total = lax.dynamic_index_in_dim(parts, row, 0, keepdims=False).astype(jnp.float32)
    for step in range(1, size):
        there = lax.dynamic_index_in_dim(parts, (row + step) % size, 0, keepdims=False)
        total = total + shift_rows(there, step).astype(jnp.float32)
    return total


def tile_kernel(blocks_ref, index_ref, band_ref, out_ref):
    band = pl.program_id(0)
    band_rows = band_ref.shape[1]
    senders, slots = out_ref.shape[0], out_ref.shape[2]
    columns = index_ref[0].T
    places = lax.broadcasted_iota(jnp.int32, (TILE, band_rows), 1)
    for sender in range(senders):
        for slot in range(slots):
            k = sender * slots + slot
            pick = jnp.where(columns[:, k : k + 1] == places, 1.0, 0.0).astype(jnp.bfloat16)
            start = pl.multiple_of(blocks_ref[band, k] * TILE, TILE)
            out_ref[sender, 0, slot] = jnp.dot(
                pick, band_ref[0, :, pl.ds(start, TILE)], preferred_element_type=jnp.float32
            ).astype(jnp.bfloat16)


def build_tiles(blocks, index, bands, row_count):
    col_count, band_rows, width = bands.shape
    return pl.pallas_call(
        tile_kernel,
        grid_spec=pltpu.PrefetchScalarGridSpec(
            num_scalar_prefetch=1,
            grid=(col_count,),
            in_specs=[
                pl.BlockSpec((1, row_count * TILE_CAP, TILE), lambda b, _: (b, 0, 0)),
                pl.BlockSpec((1, band_rows, width), lambda b, _: (b, 0, 0)),
            ],
            out_specs=pl.BlockSpec(
                (row_count, 1, TILE_CAP, TILE, TILE), lambda b, _: (0, b, 0, 0, 0)
            ),
        ),
        out_shape=jax.ShapeDtypeStruct(
            (row_count, col_count, TILE_CAP, TILE, TILE), jnp.bfloat16
        ),
        compiler_params=pltpu.CompilerParams(vmem_limit_bytes=32 * 1024 * 1024),
        cost_estimate=pl.CostEstimate(
            flops=2 * 256 * TILE * TILE * band_rows, bytes_accessed=25_000_000, transcendentals=0
        ),
    )(blocks, index, bands)


def route_indices(tile_owner, tile_rows, tile_block, tile_count, device_count):
    tile_total = tile_rows.shape[0]
    owners = tile_owner[:, 0]
    order_ids = jnp.arange(tile_total, dtype=jnp.int32)
    live = order_ids < tile_count[0]
    earlier = (
        (owners[:, None] == owners[None, :])
        & live[None, :]
        & (order_ids[None, :] < order_ids[:, None])
    )
    slots = jnp.sum(earlier.astype(jnp.int32), axis=1)
    dump = device_count * TILE_CAP
    target = jnp.where(live, owners * TILE_CAP + slots, dump)
    table = (target[None, :] == jnp.arange(dump, dtype=jnp.int32)[:, None]).astype(jnp.float32)
    coded = jnp.where(tile_rows >= 0, tile_rows + 1 + CODE * tile_block[:, None], 0)
    placed = precise(table, coded.astype(jnp.float32))
    sent = placed.reshape(device_count, TILE_CAP, TILE)
    return lax.all_to_all(sent, ("row", "col"), split_axis=0, concat_axis=0, tiled=True)


def shards(
    trailing,
    first_panel,
    first_gram,
    second_panel,
    second_lead,
    second_gram,
    tile_owner,
    tile_rows,
    tile_block,
    tile_count,
):
    row_count = lax.axis_size("row")
    col_count = lax.axis_size("col")
    row_index = lax.axis_index("row")
    col_index = lax.axis_index("col")
    device_count = row_count * col_count
    part_rows = first_panel.shape[0]
    gram_rows = P_SIZE // col_count
    low = jnp.bfloat16

    panels = jnp.concatenate(
        [first_panel, second_panel - precise(first_panel, second_lead)], axis=1
    ).astype(low)
    gathered = lax.all_gather(panels, "col", axis=0, tiled=True)

    perm = []
    for there in range(device_count):
        row, col = divmod(there, col_count)
        perm.append((col * row_count + row, there))
    own = spread_rows(lax.ppermute(panels, ("row", "col"), perm)).reshape(-1, 2 * P_SIZE)

    coded = route_indices(tile_owner, tile_rows, tile_block, tile_count, device_count)
    coded = coded.astype(jnp.int32).reshape(row_count, col_count, TILE_CAP, TILE)
    coded = coded.transpose(1, 0, 2, 3).reshape(col_count, row_count * TILE_CAP, TILE)
    index = coded % CODE - 1
    blocks = coded[:, :, 0] // CODE

    product = -contract_rows(trailing.astype(low), gathered)
    mine = sum_rows(product.astype(low).reshape(row_count, part_rows, 2 * P_SIZE))
    columns = spread_rows(mine.astype(low)).reshape(-1, 2 * P_SIZE)
    first_column = columns[:, :P_SIZE].astype(jnp.float32)
    second_low = columns[:, P_SIZE:]
    second_column = second_low.astype(jnp.float32)

    bands = lax.all_gather(second_low, "col", axis=0, tiled=False)
    tiles = build_tiles(blocks, index, bands, row_count)
    child_tiles = tiles.reshape(device_count * TILE_CAP, TILE, TILE)

    width = P_SIZE // row_count
    start = row_index * width
    first_part = lax.dynamic_slice_in_dim(columns, start, width, 1)
    second_part = lax.dynamic_slice_in_dim(columns, P_SIZE + start, width, 1)
    against_first = contract_rows(own[:, :P_SIZE], jnp.concatenate([first_part, second_part], 1))
    against_second = contract_rows(own[:, P_SIZE:], second_part)
    sums = jnp.concatenate([against_first, against_second], axis=1).astype(low)
    sums = sums.reshape(col_count, gram_rows, 3 * width)
    sums = lax.all_to_all(sums, "col", split_axis=0, concat_axis=0, tiled=True)
    sums = jnp.sum(sums.astype(jnp.float32), axis=0)
    sums = spread_rows(sums).reshape(row_count, gram_rows, 3, width)
    sums = sums.transpose(2, 1, 0, 3).reshape(3, gram_rows, P_SIZE)

    gram_start = col_index * gram_rows
    gram_part = lax.dynamic_slice_in_dim(first_gram, gram_start, gram_rows, 0)
    lead_part = lax.dynamic_slice_in_dim(second_lead, gram_start, gram_rows, 1)
    first_corner = gram_part - sums[0]
    second_upper = -(precise(gram_part, second_lead) + sums[1])
    second_corner = (
        lax.dynamic_slice_in_dim(second_gram, gram_start, gram_rows, 0)
        + precise(precise(lead_part.T, first_gram), second_lead)
        - sums[2]
    )
    return (first_column, first_corner, second_upper, second_column, second_corner, child_tiles)


def solution(mesh):
    in_specs = (
        P("row", "col"),
        P(("row", "col"), None),
        P(),
        P(("row", "col"), None),
        P(),
        P(),
        P(("row", "col"), None),
        P(("row", "col"), None),
        P(("row", "col")),
        P(("row", "col")),
    )
    out_specs = (
        P("col", None),
        P("col", None),
        P("col", None),
        P("col", None),
        P("col", None),
        P(("row", "col"), None, None),
    )
    return jax.shard_map(shards, mesh=mesh, in_specs=in_specs, out_specs=out_specs, check_vma=False)
```

```python
import functools

import jax
import jax.numpy as jnp
from jax import lax
from jax.experimental import pallas as pl
from jax.experimental.pallas import tpu as pltpu
from jax.sharding import PartitionSpec as P

P_SIZE = 512
TILE = 128
TILE_CAP = 2
SIDE = 4
CODE = 512


def precise(left, right):
    return jnp.dot(left, right, precision=lax.Precision.HIGHEST, preferred_element_type=jnp.float32)


def contract_rows(left, right):
    return lax.dot_general(
        left, right, (((0,), (0,)), ((), ())), preferred_element_type=jnp.float32
    )


def place(block, received, index, dim):
    size = len(received) + 1
    shape = block.shape[:dim] + (size,) + block.shape[dim:]
    out = jnp.zeros(shape, block.dtype)
    out = lax.dynamic_update_index_in_dim(out, block, index, dim)
    for step, value in received:
        out = lax.dynamic_update_index_in_dim(out, value, (index - step) % size, dim)
    return out


def shift_rows(value, step):
    size = lax.axis_size("row")
    return lax.ppermute(value, "row", [(i, (i + step) % size) for i in range(size)])


def spread_rows(block):
    size = lax.axis_size("row")
    received = [(step, shift_rows(block, step)) for step in range(1, size)]
    return place(block, received, lax.axis_index("row"), 0)


def sum_rows(parts):
    size = lax.axis_size("row")
    row = lax.axis_index("row")
    total = lax.dynamic_index_in_dim(parts, row, 0, keepdims=False).astype(jnp.float32)
    for step in range(1, size):
        there = lax.dynamic_index_in_dim(parts, (row + step) % size, 0, keepdims=False)
        total = total + shift_rows(there, step).astype(jnp.float32)
    return total


def shift_chips(value, dim, step):
    perm = []
    for col in range(lax.axis_size("col")):
        place_of = [col // (2 * SIDE), col // 2 % SIDE, col % 2]
        place_of[dim] = (place_of[dim] + step) % SIDE
        perm.append((col, (place_of[0] * SIDE + place_of[1]) * 2 + place_of[2]))
    return lax.ppermute(value, "col", perm)


def spread_chips(block, dim, at):
    col = lax.axis_index("col")
    index = col // (2 * SIDE) if dim == 0 else col // 2 % SIDE
    received = [(step, shift_chips(block, dim, step)) for step in range(1, SIDE)]
    return place(block, received, index, at)


def spread_cores(block, at):
    size = lax.axis_size("col")
    other = lax.ppermute(block, "col", [(i, i ^ 1) for i in range(size)])
    return place(block, [(1, other)], lax.axis_index("col") % 2, at)


def spread_cols(block):
    half = block.shape[1] // 2
    left = spread_chips(spread_chips(block[:, :half], 1, 0), 0, 0)
    right = spread_chips(spread_chips(block[:, half:], 0, 0), 1, 1)
    return spread_cores(left, 2), spread_cores(right, 2)


def tile_kernel(blocks_ref, index_ref, band_ref, out_ref):
    pieces, group, piece_rows = band_ref.shape[:3]
    senders, _, slots = out_ref.shape[:3]
    first = pl.program_id(0) * group
    places = lax.broadcasted_iota(jnp.int32, (TILE, pieces * piece_rows), 1)
    for band in range(group):
        columns = index_ref[band].T
        for sender in range(senders):
            for slot in range(slots):
                k = sender * slots + slot
                pick = jnp.where(columns[:, k : k + 1] == places, 1.0, 0.0).astype(jnp.bfloat16)
                start = pl.multiple_of(blocks_ref[first + band, k] * TILE, TILE)
                rows = [band_ref[piece, band, :, pl.ds(start, TILE)] for piece in range(pieces)]
                out_ref[sender, band, slot] = jnp.dot(
                    pick, jnp.concatenate(rows, axis=0), preferred_element_type=jnp.float32
                ).astype(jnp.bfloat16)


def build_tiles(blocks, index, bands):
    pieces, col_count, piece_rows, width = bands.shape
    row_count = index.shape[1] // TILE_CAP
    group = 8
    return pl.pallas_call(
        tile_kernel,
        grid_spec=pltpu.PrefetchScalarGridSpec(
            num_scalar_prefetch=1,
            grid=(col_count // group,),
            in_specs=[
                pl.BlockSpec((group, row_count * TILE_CAP, TILE), lambda b, _: (b, 0, 0)),
                pl.BlockSpec((pieces, group, piece_rows, width), lambda b, _: (0, b, 0, 0)),
            ],
            out_specs=pl.BlockSpec(
                (row_count, group, TILE_CAP, TILE, TILE), lambda b, _: (0, b, 0, 0, 0)
            ),
        ),
        out_shape=jax.ShapeDtypeStruct(
            (row_count, col_count, TILE_CAP, TILE, TILE), jnp.bfloat16
        ),
        compiler_params=pltpu.CompilerParams(vmem_limit_bytes=56 * 1024 * 1024),
        cost_estimate=pl.CostEstimate(
            flops=512 * TILE * TILE * pieces * piece_rows,
            bytes_accessed=25_000_000,
            transcendentals=0,
        ),
    )(blocks, index, bands)


def route_indices(tile_owner, tile_rows, tile_block, tile_count, device_count):
    tile_total = tile_rows.shape[0]
    owners = tile_owner[:, 0]
    order_ids = jnp.arange(tile_total, dtype=jnp.int32)
    live = order_ids < tile_count[0]
    earlier = (
        (owners[:, None] == owners[None, :])
        & live[None, :]
        & (order_ids[None, :] < order_ids[:, None])
    )
    slots = jnp.sum(earlier.astype(jnp.int32), axis=1)
    dump = device_count * TILE_CAP
    target = jnp.where(live, owners * TILE_CAP + slots, dump)
    table = (target[None, :] == jnp.arange(dump, dtype=jnp.int32)[:, None]).astype(jnp.float32)
    coded = jnp.where(tile_rows >= 0, tile_rows + 1 + CODE * tile_block[:, None], 0)
    placed = precise(table, coded.astype(jnp.float32))
    return placed.reshape(device_count, TILE_CAP, TILE)


def shards(
    trailing,
    first_panel,
    first_gram,
    second_panel,
    second_lead,
    second_gram,
    tile_owner,
    tile_rows,
    tile_block,
    tile_count,
):
    row_count = lax.axis_size("row")
    col_count = lax.axis_size("col")
    row_index = lax.axis_index("row")
    col_index = lax.axis_index("col")
    device_count = row_count * col_count
    part_rows = first_panel.shape[0]
    gram_rows = P_SIZE // col_count
    low = jnp.bfloat16

    rest = (second_panel - precise(first_panel, second_lead)).astype(low)
    left, right = spread_cols(rest)
    first_low, _ = lax.optimization_barrier((first_panel.astype(low), rest))
    first_rows = lax.all_gather(first_low, "col", axis=0, tiled=True)

    perm = []
    for there in range(device_count):
        row, col = divmod(there, col_count)
        perm.append((col * row_count + row, there))
    own = lax.ppermute(jnp.concatenate([first_low, rest], axis=1), ("row", "col"), perm)

    trailing_low = lax.optimization_barrier(trailing.astype(low))

    def product(*factors):
        parts = [-contract_rows(trailing_low, f.reshape(-1, f.shape[-1])) for f in factors]
        whole = jnp.concatenate(parts, axis=1) if len(parts) > 1 else parts[0]
        return whole.astype(low).reshape(row_count, part_rows, P_SIZE)

    second_part = sum_rows(product(left, right)).astype(low)
    second_low = spread_rows(second_part).reshape(-1, P_SIZE)
    second_column = second_low.astype(jnp.float32)
    bands = lax.all_gather(second_low, "col", axis=0, tiled=False)

    first_rows, own, _ = lax.optimization_barrier((first_rows, own, second_low))
    lists = route_indices(tile_owner, tile_rows, tile_block, tile_count, device_count)
    first_product, lists = lax.optimization_barrier((product(first_rows), lists))
    first_part = sum_rows(first_product).astype(low)
    coded = lax.all_to_all(lists, ("row", "col"), split_axis=0, concat_axis=0, tiled=True)
    first_low_column = spread_rows(first_part).reshape(-1, P_SIZE)
    first_column = first_low_column.astype(jnp.float32)
    own = spread_rows(own).reshape(-1, 2 * P_SIZE)

    gram_start = col_index * gram_rows
    gram_part = lax.dynamic_slice_in_dim(first_gram, gram_start, gram_rows, 0)
    lead_part = lax.dynamic_slice_in_dim(second_lead, gram_start, gram_rows, 1)
    upper_part = precise(gram_part, second_lead)
    corner_part = lax.dynamic_slice_in_dim(second_gram, gram_start, gram_rows, 0) + precise(
        precise(lead_part.T, first_gram), second_lead
    )

    width = P_SIZE // row_count
    start = row_index * width
    first_cut = lax.dynamic_slice_in_dim(first_low_column, start, width, 1)
    second_cut = lax.dynamic_slice_in_dim(second_low, start, width, 1)
    against_first = contract_rows(
        own[:, :P_SIZE], jnp.concatenate([first_cut, second_cut], axis=1)
    )
    against_second = contract_rows(own[:, P_SIZE:], second_cut)
    sums = jnp.concatenate([against_first, against_second], axis=1).astype(low)
    sums = sums.reshape(col_count, gram_rows, 3 * width)
    sums = lax.all_to_all(sums, "col", split_axis=0, concat_axis=0, tiled=True)
    sums = jnp.sum(sums.astype(jnp.float32), axis=0)
    bands, sums, upper_part, corner_part = lax.optimization_barrier(
        (bands, sums, upper_part, corner_part)
    )
    sums = spread_rows(sums).reshape(row_count, gram_rows, 3, width)
    sums = sums.transpose(1, 2, 0, 3).reshape(gram_rows, 3 * P_SIZE)

    coded = coded.astype(jnp.int32).reshape(row_count, col_count, TILE_CAP, TILE)
    coded = coded.transpose(1, 0, 2, 3).reshape(col_count, row_count * TILE_CAP, TILE)
    tiles = build_tiles(coded[:, :, 0] // CODE, coded % CODE - 1, bands[None])
    child_tiles = tiles.reshape(device_count * TILE_CAP, TILE, TILE)

    first_corner = gram_part - sums[:, :P_SIZE]
    second_upper = -(upper_part + sums[:, P_SIZE : 2 * P_SIZE])
    second_corner = corner_part - sums[:, 2 * P_SIZE :]
    return (first_column, first_corner, second_upper, second_column, second_corner, child_tiles)


def solution(mesh):
    in_specs = (
        P("row", "col"),
        P(("row", "col"), None),
        P(),
        P(("row", "col"), None),
        P(),
        P(),
        P(("row", "col"), None),
        P(("row", "col"), None),
        P(("row", "col")),
        P(("row", "col")),
    )
    out_specs = (
        P("col", None),
        P("col", None),
        P("col", None),
        P("col", None),
        P("col", None),
        P(("row", "col"), None, None),
    )
    return jax.shard_map(shards, mesh=mesh, in_specs=in_specs, out_specs=out_specs, check_vma=False)
```

```python
import functools

import jax
import jax.numpy as jnp
from jax import lax
from jax.experimental import pallas as pl
from jax.experimental.pallas import tpu as pltpu
from jax.sharding import PartitionSpec as P

P_SIZE = 512
TILE = 128
TILE_CAP = 2
SIDE = 4
CODE = 512


def precise(left, right):
    return jnp.dot(left, right, precision=lax.Precision.HIGHEST, preferred_element_type=jnp.float32)


def contract_rows(left, right):
    return lax.dot_general(
        left, right, (((0,), (0,)), ((), ())), preferred_element_type=jnp.float32
    )


def after(value, *others):
    return lax.optimization_barrier((value, *others))[0]


def place(block, received, index, dim):
    size = len(received) + 1
    shape = block.shape[:dim] + (size,) + block.shape[dim:]
    out = jnp.zeros(shape, block.dtype)
    out = lax.dynamic_update_index_in_dim(out, block, index, dim)
    for step, value in received:
        out = lax.dynamic_update_index_in_dim(out, value, (index - step) % size, dim)
    return out


def shift_rows(value, step):
    size = lax.axis_size("row")
    return lax.ppermute(value, "row", [(i, (i + step) % size) for i in range(size)])


def exchange_rows(block):
    return [block] + [shift_rows(block, step) for step in range(1, lax.axis_size("row"))]


def in_row_order(blocks):
    return place(blocks[0], list(enumerate(blocks))[1:], lax.axis_index("row"), 0)


def sum_rows(parts):
    size = lax.axis_size("row")
    row = lax.axis_index("row")
    total = lax.dynamic_index_in_dim(parts, row, 0, keepdims=False).astype(jnp.float32)
    for step in range(1, size):
        there = lax.dynamic_index_in_dim(parts, (row + step) % size, 0, keepdims=False)
        total = total + shift_rows(there, step).astype(jnp.float32)
    return total


def shift_chips(value, dim, step):
    perm = []
    for col in range(lax.axis_size("col")):
        place_of = [col // (2 * SIDE), col // 2 % SIDE, col % 2]
        place_of[dim] = (place_of[dim] + step) % SIDE
        perm.append((col, (place_of[0] * SIDE + place_of[1]) * 2 + place_of[2]))
    return lax.ppermute(value, "col", perm)


def spread_chips(block, dim, at):
    col = lax.axis_index("col")
    index = col // (2 * SIDE) if dim == 0 else col // 2 % SIDE
    received = [(step, shift_chips(block, dim, step)) for step in range(1, SIDE)]
    return place(block, received, index, at)


def spread_cores(block, at):
    size = lax.axis_size("col")
    other = lax.ppermute(block, "col", [(i, i ^ 1) for i in range(size)])
    return place(block, [(1, other)], lax.axis_index("col") % 2, at)


def spread_lines(block):
    half = block.shape[1] // 2
    return spread_chips(block[:, :half], 1, 0), spread_chips(block[:, half:], 0, 0)


def tile_kernel(blocks_ref, index_ref, band_ref, out_ref):
    group, band_rows = band_ref.shape[:2]
    senders, _, slots = out_ref.shape[:3]
    first = pl.program_id(0) * group
    places = lax.broadcasted_iota(jnp.int32, (band_rows, TILE), 0)
    for band in range(group):
        for sender in range(senders):
            for slot in range(slots):
                k = sender * slots + slot
                pick = jnp.where(index_ref[band, k : k + 1] == places, 1.0, 0.0)
                start = pl.multiple_of(blocks_ref[first + band, k] * TILE, TILE)
                out_ref[sender, band, slot] = contract_rows(
                    pick.astype(jnp.bfloat16), band_ref[band, :, pl.ds(start, TILE)]
                ).astype(jnp.bfloat16)


def build_tiles(blocks, index, bands):
    col_count, band_rows, width = bands.shape
    row_count = index.shape[1] // TILE_CAP
    group = 8
    return pl.pallas_call(
        tile_kernel,
        grid_spec=pltpu.PrefetchScalarGridSpec(
            num_scalar_prefetch=1,
            grid=(col_count // group,),
            in_specs=[
                pl.BlockSpec((group, row_count * TILE_CAP, TILE), lambda b, _: (b, 0, 0)),
                pl.BlockSpec((group, band_rows, width), lambda b, _: (b, 0, 0)),
            ],
            out_specs=pl.BlockSpec(
                (row_count, group, TILE_CAP, TILE, TILE), lambda b, _: (0, b, 0, 0, 0)
            ),
        ),
        out_shape=jax.ShapeDtypeStruct(
            (row_count, col_count, TILE_CAP, TILE, TILE), jnp.bfloat16
        ),
        compiler_params=pltpu.CompilerParams(vmem_limit_bytes=56 * 1024 * 1024),
        cost_estimate=pl.CostEstimate(
            flops=512 * TILE * TILE * band_rows,
            bytes_accessed=25_000_000,
            transcendentals=0,
        ),
    )(blocks, index, bands)


def route_indices(tile_owner, tile_rows, tile_block, tile_count, device_count):
    tile_total = tile_rows.shape[0]
    owners = tile_owner[:, 0]
    order_ids = jnp.arange(tile_total, dtype=jnp.int32)
    live = order_ids < tile_count[0]
    earlier = (
        (owners[:, None] == owners[None, :])
        & live[None, :]
        & (order_ids[None, :] < order_ids[:, None])
    )
    slots = jnp.sum(earlier.astype(jnp.int32), axis=1)
    dump = device_count * TILE_CAP
    target = jnp.where(live, owners * TILE_CAP + slots, dump)
    table = (target[None, :] == jnp.arange(dump, dtype=jnp.int32)[:, None]).astype(jnp.float32)
    coded = jnp.where(tile_rows >= 0, tile_rows + 1 + CODE * tile_block[:, None], 0)
    placed = precise(table, coded.astype(jnp.float32))
    return placed.reshape(device_count, TILE_CAP, TILE)


def shards(
    trailing,
    first_panel,
    first_gram,
    second_panel,
    second_lead,
    second_gram,
    tile_owner,
    tile_rows,
    tile_block,
    tile_count,
):
    row_count = lax.axis_size("row")
    col_count = lax.axis_size("col")
    row_index = lax.axis_index("row")
    col_index = lax.axis_index("col")
    device_count = row_count * col_count
    part_rows = first_panel.shape[0]
    gram_rows = P_SIZE // col_count
    low = jnp.bfloat16

    rest = (second_panel - precise(first_panel, second_lead)).astype(low)
    left, right = spread_lines(rest)
    first_low = after(first_panel, left).astype(low)
    first_rows = lax.all_gather(first_low, "col", axis=0, tiled=True)
    left = spread_chips(left, 0, 0)
    right = spread_chips(right, 1, 1)
    right, trailing_low = lax.optimization_barrier((right, after(trailing, left).astype(low)))
    left, right = spread_cores(left, 2), spread_cores(right, 2)

    def product(*factors):
        parts = [-contract_rows(trailing_low, f.reshape(-1, f.shape[-1])) for f in factors]
        whole = jnp.concatenate(parts, axis=1) if len(parts) > 1 else parts[0]
        return whole.astype(low).reshape(row_count, part_rows, P_SIZE)

    second_part = sum_rows(product(left, right)).astype(low)
    second_blocks = exchange_rows(second_part)
    second_low = in_row_order(second_blocks).reshape(-1, P_SIZE)
    bands = lax.all_gather(second_low, "col", axis=0, tiled=False)

    perm = []
    for there in range(device_count):
        row, col = divmod(there, col_count)
        perm.append((col * row_count + row, there))
    own = after(jnp.concatenate([first_low, rest], axis=1), second_part)
    own = lax.ppermute(own, ("row", "col"), perm)

    lists = route_indices(tile_owner, tile_rows, tile_block, tile_count, device_count)
    first_product = product(after(first_rows, second_part))
    first_product, lists = lax.optimization_barrier((first_product, lists))
    first_part = sum_rows(first_product).astype(low)
    coded = lax.all_to_all(lists, ("row", "col"), split_axis=0, concat_axis=0, tiled=True)
    own = jnp.concatenate(exchange_rows(after(own, first_product)), axis=0)
    first_blocks = exchange_rows(first_part)

    width = P_SIZE // row_count
    start = row_index * width
    cuts = [
        jnp.concatenate([lax.dynamic_slice_in_dim(b, start, width, 1) for b in blocks], axis=0)
        for blocks in (first_blocks, second_blocks)
    ]
    against_first = contract_rows(own[:, :P_SIZE], jnp.concatenate(cuts, axis=1))
    against_second = contract_rows(own[:, P_SIZE:], cuts[1])
    sums = jnp.concatenate([against_first, against_second], axis=1).astype(low)
    sums = sums.reshape(col_count, gram_rows, 3 * width)
    first_column = in_row_order(after(first_blocks, sums)).reshape(-1, P_SIZE).astype(jnp.float32)
    second_column = after(second_low, sums).astype(jnp.float32)

    lead = after(second_lead, sums)
    gram_start = col_index * gram_rows
    gram_part = lax.dynamic_slice_in_dim(first_gram, gram_start, gram_rows, 0)
    lead_part = lax.dynamic_slice_in_dim(lead, gram_start, gram_rows, 1)
    upper_part = precise(gram_part, lead)
    corner_part = lax.dynamic_slice_in_dim(second_gram, gram_start, gram_rows, 0) + precise(
        precise(lead_part.T, first_gram), lead
    )

    sums = lax.all_to_all(sums, "col", split_axis=0, concat_axis=0, tiled=True)
    sums = jnp.sum(sums.astype(jnp.float32), axis=0)
    bands, sums, upper_part, corner_part = lax.optimization_barrier(
        (bands, sums, upper_part, corner_part)
    )
    sums = in_row_order(exchange_rows(sums)).reshape(row_count, gram_rows, 3, width)
    sums = sums.transpose(1, 2, 0, 3).reshape(gram_rows, 3 * P_SIZE)

    coded = coded.astype(jnp.int32).reshape(row_count, col_count, TILE_CAP, TILE)
    coded = coded.transpose(1, 0, 2, 3).reshape(col_count, row_count * TILE_CAP, TILE)
    tiles = build_tiles(coded[:, :, 0] // CODE, coded % CODE - 1, bands)
    child_tiles = tiles.reshape(device_count * TILE_CAP, TILE, TILE)

    first_corner = gram_part - sums[:, :P_SIZE]
    second_upper = -(upper_part + sums[:, P_SIZE : 2 * P_SIZE])
    second_corner = corner_part - sums[:, 2 * P_SIZE :]
    return (first_column, first_corner, second_upper, second_column, second_corner, child_tiles)


def solution(mesh):
    in_specs = (
        P("row", "col"),
        P(("row", "col"), None),
        P(),
        P(("row", "col"), None),
        P(),
        P(),
        P(("row", "col"), None),
        P(("row", "col"), None),
        P(("row", "col")),
        P(("row", "col")),
    )
    out_specs = (
        P("col", None),
        P("col", None),
        P("col", None),
        P("col", None),
        P("col", None),
        P(("row", "col"), None, None),
    )
    return jax.shard_map(shards, mesh=mesh, in_specs=in_specs, out_specs=out_specs, check_vma=False)
```

```python
import functools

import jax
import jax.numpy as jnp
from jax import lax
from jax.experimental import pallas as pl
from jax.experimental.pallas import tpu as pltpu
from jax.sharding import PartitionSpec as P

P_SIZE = 512
TILE = 128
TILE_CAP = 2
SIDE = 4
CODE = 512


def precise(left, right):
    return jnp.dot(left, right, precision=lax.Precision.HIGHEST, preferred_element_type=jnp.float32)


def contract_rows(left, right):
    return lax.dot_general(
        left, right, (((0,), (0,)), ((), ())), preferred_element_type=jnp.float32
    )


def after(value, *others):
    return lax.optimization_barrier((value, *others))[0]


def place(block, received, index, dim):
    size = len(received) + 1
    shape = block.shape[:dim] + (size,) + block.shape[dim:]
    out = jnp.zeros(shape, block.dtype)
    out = lax.dynamic_update_index_in_dim(out, block, index, dim)
    for step, value in received:
        out = lax.dynamic_update_index_in_dim(out, value, (index - step) % size, dim)
    return out


def shift_rows(value, step):
    size = lax.axis_size("row")
    return lax.ppermute(value, "row", [(i, (i + step) % size) for i in range(size)])


def exchange_rows(block):
    return [block] + [shift_rows(block, step) for step in range(1, lax.axis_size("row"))]


def in_row_order(blocks):
    return place(blocks[0], list(enumerate(blocks))[1:], lax.axis_index("row"), 0)


def sum_rows(parts):
    size = lax.axis_size("row")
    row = lax.axis_index("row")
    total = lax.dynamic_index_in_dim(parts, row, 0, keepdims=False).astype(jnp.float32)
    for step in range(1, size):
        there = lax.dynamic_index_in_dim(parts, (row + step) % size, 0, keepdims=False)
        total = total + shift_rows(there, step).astype(jnp.float32)
    return total


def shift_chips(value, dim, step):
    perm = []
    for col in range(lax.axis_size("col")):
        place_of = [col // (2 * SIDE), col // 2 % SIDE, col % 2]
        place_of[dim] = (place_of[dim] + step) % SIDE
        perm.append((col, (place_of[0] * SIDE + place_of[1]) * 2 + place_of[2]))
    return lax.ppermute(value, "col", perm)


def spread_chips(block, dim, at):
    col = lax.axis_index("col")
    index = col // (2 * SIDE) if dim == 0 else col // 2 % SIDE
    received = [(step, shift_chips(block, dim, step)) for step in range(1, SIDE)]
    return place(block, received, index, at)


def spread_cores(block, at):
    size = lax.axis_size("col")
    other = lax.ppermute(block, "col", [(i, i ^ 1) for i in range(size)])
    return place(block, [(1, other)], lax.axis_index("col") % 2, at)


def spread_lines(block):
    half = block.shape[1] // 2
    return spread_chips(block[:, :half], 1, 0), spread_chips(block[:, half:], 0, 0)


def tile_kernel(blocks_ref, index_ref, band_ref, out_ref):
    group, band_rows = band_ref.shape[:2]
    senders, _, slots = out_ref.shape[:3]
    first = pl.program_id(0) * group
    places = lax.broadcasted_iota(jnp.int32, (band_rows, TILE), 0)
    for band in range(group):
        for sender in range(senders):
            for slot in range(slots):
                k = sender * slots + slot
                pick = jnp.where(index_ref[band, k : k + 1] == places, 1.0, 0.0)
                start = pl.multiple_of(blocks_ref[first + band, k] * TILE, TILE)
                out_ref[sender, band, slot] = contract_rows(
                    pick.astype(jnp.bfloat16), band_ref[band, :, pl.ds(start, TILE)]
                ).astype(jnp.bfloat16)


def build_tiles(blocks, index, bands):
    col_count, band_rows, width = bands.shape
    row_count = index.shape[1] // TILE_CAP
    group = 8
    return pl.pallas_call(
        tile_kernel,
        grid_spec=pltpu.PrefetchScalarGridSpec(
            num_scalar_prefetch=1,
            grid=(col_count // group,),
            in_specs=[
                pl.BlockSpec((group, row_count * TILE_CAP, TILE), lambda b, _: (b, 0, 0)),
                pl.BlockSpec((group, band_rows, width), lambda b, _: (b, 0, 0)),
            ],
            out_specs=pl.BlockSpec(
                (row_count, group, TILE_CAP, TILE, TILE), lambda b, _: (0, b, 0, 0, 0)
            ),
        ),
        out_shape=jax.ShapeDtypeStruct(
            (row_count, col_count, TILE_CAP, TILE, TILE), jnp.bfloat16
        ),
        compiler_params=pltpu.CompilerParams(vmem_limit_bytes=56 * 1024 * 1024),
        cost_estimate=pl.CostEstimate(
            flops=512 * TILE * TILE * band_rows,
            bytes_accessed=25_000_000,
            transcendentals=0,
        ),
    )(blocks, index, bands)


def route_indices(tile_owner, tile_rows, tile_block, tile_count, device_count):
    tile_total = tile_rows.shape[0]
    owners = tile_owner[:, 0]
    order_ids = jnp.arange(tile_total, dtype=jnp.int32)
    live = order_ids < tile_count[0]
    earlier = (
        (owners[:, None] == owners[None, :])
        & live[None, :]
        & (order_ids[None, :] < order_ids[:, None])
    )
    slots = jnp.sum(earlier.astype(jnp.int32), axis=1)
    dump = device_count * TILE_CAP
    target = jnp.where(live, owners * TILE_CAP + slots, dump)
    table = (target[None, :] == jnp.arange(dump, dtype=jnp.int32)[:, None]).astype(jnp.float32)
    coded = jnp.where(tile_rows >= 0, tile_rows + 1 + CODE * tile_block[:, None], 0)
    placed = precise(table, coded.astype(jnp.float32))
    return placed.reshape(device_count, TILE_CAP, TILE)


def shards(
    trailing,
    first_panel,
    first_gram,
    second_panel,
    second_lead,
    second_gram,
    tile_owner,
    tile_rows,
    tile_block,
    tile_count,
):
    row_count = lax.axis_size("row")
    col_count = lax.axis_size("col")
    row_index = lax.axis_index("row")
    col_index = lax.axis_index("col")
    device_count = row_count * col_count
    part_rows = first_panel.shape[0]
    gram_rows = P_SIZE // col_count
    low = jnp.bfloat16

    share = jnp.dot(
        first_panel,
        second_lead,
        precision=lax.Precision.HIGH,
        preferred_element_type=jnp.float32,
    )
    rest = (second_panel - share).astype(low)
    left, right = spread_lines(rest)
    first_low = after(first_panel, left).astype(low)
    first_rows = lax.all_gather(first_low, "col", axis=0, tiled=True)
    left = spread_chips(left, 0, 0)
    right = spread_chips(right, 1, 1)
    right, trailing_low = lax.optimization_barrier((right, after(trailing, left).astype(low)))
    left, right = spread_cores(left, 2), spread_cores(right, 2)

    def product(*factors):
        parts = [-contract_rows(trailing_low, f.reshape(-1, f.shape[-1])) for f in factors]
        whole = jnp.concatenate(parts, axis=1) if len(parts) > 1 else parts[0]
        return whole.astype(low).reshape(row_count, part_rows, P_SIZE)

    second_part = sum_rows(product(left, right)).astype(low)
    second_blocks = exchange_rows(second_part)
    second_low = in_row_order(second_blocks).reshape(-1, P_SIZE)
    bands = lax.all_gather(second_low, "col", axis=0, tiled=False)

    perm = []
    for there in range(device_count):
        row, col = divmod(there, col_count)
        perm.append((col * row_count + row, there))
    own = after(jnp.concatenate([first_low, rest], axis=1), second_part)
    own = lax.ppermute(own, ("row", "col"), perm)

    lists = route_indices(tile_owner, tile_rows, tile_block, tile_count, device_count)
    first_product = product(after(first_rows, second_part))
    first_product, lists = lax.optimization_barrier((first_product, lists))
    first_part = sum_rows(first_product).astype(low)
    coded = lax.all_to_all(lists, ("row", "col"), split_axis=0, concat_axis=0, tiled=True)
    own = jnp.concatenate(exchange_rows(after(own, first_product)), axis=0)
    first_blocks = exchange_rows(first_part)

    width = P_SIZE // row_count
    start = row_index * width
    cuts = [
        jnp.concatenate([lax.dynamic_slice_in_dim(b, start, width, 1) for b in blocks], axis=0)
        for blocks in (first_blocks, second_blocks)
    ]
    against_first = contract_rows(own[:, :P_SIZE], jnp.concatenate(cuts, axis=1))
    against_second = contract_rows(own[:, P_SIZE:], cuts[1])
    sums = jnp.concatenate([against_first, against_second], axis=1).astype(low)
    sums = sums.reshape(col_count, gram_rows, 3 * width)
    first_column = in_row_order(after(first_blocks, sums)).reshape(-1, P_SIZE).astype(jnp.float32)
    second_column = after(second_low, sums).astype(jnp.float32)

    lead = after(second_lead, sums)
    gram_start = col_index * gram_rows
    gram_part = lax.dynamic_slice_in_dim(first_gram, gram_start, gram_rows, 0)
    lead_part = lax.dynamic_slice_in_dim(lead, gram_start, gram_rows, 1)
    upper_part = precise(gram_part, lead)
    corner_part = lax.dynamic_slice_in_dim(second_gram, gram_start, gram_rows, 0) + precise(
        precise(lead_part.T, first_gram), lead
    )

    sums = lax.all_to_all(sums, "col", split_axis=0, concat_axis=0, tiled=True)
    sums = jnp.sum(sums.astype(jnp.float32), axis=0)
    bands, sums, upper_part, corner_part = lax.optimization_barrier(
        (bands, sums, upper_part, corner_part)
    )
    sums = in_row_order(exchange_rows(sums)).reshape(row_count, gram_rows, 3, width)
    sums = sums.transpose(1, 2, 0, 3).reshape(gram_rows, 3 * P_SIZE)

    coded = coded.astype(jnp.int32).reshape(row_count, col_count, TILE_CAP, TILE)
    coded = coded.transpose(1, 0, 2, 3).reshape(col_count, row_count * TILE_CAP, TILE)
    tiles = build_tiles(coded[:, :, 0] // CODE, coded % CODE - 1, bands)
    child_tiles = tiles.reshape(device_count * TILE_CAP, TILE, TILE)

    first_corner = gram_part - sums[:, :P_SIZE]
    second_upper = -(upper_part + sums[:, P_SIZE : 2 * P_SIZE])
    second_corner = corner_part - sums[:, 2 * P_SIZE :]
    return (first_column, first_corner, second_upper, second_column, second_corner, child_tiles)


def solution(mesh):
    in_specs = (
        P("row", "col"),
        P(("row", "col"), None),
        P(),
        P(("row", "col"), None),
        P(),
        P(),
        P(("row", "col"), None),
        P(("row", "col"), None),
        P(("row", "col")),
        P(("row", "col")),
    )
    out_specs = (
        P("col", None),
        P("col", None),
        P("col", None),
        P("col", None),
        P("col", None),
        P(("row", "col"), None, None),
    )
    return jax.shard_map(shards, mesh=mesh, in_specs=in_specs, out_specs=out_specs, check_vma=False)
```
